256 devices in a mesh: section: 32 (over z, y_lo, core), dp: 8 (over x, y_hi).
Axes of the slice: x: 4, y: 4 (y_hi: 2, y_lo: 2; y = y_hi * 2 + y_lo), z: 8, core: 2. Of those that a mesh axis runs over, the one named last changes fastest.
Arguments:
- handoff: bfloat16 [32, 2048, 4096], P('section', 'dp'), may hold values from -6 to 6
- grad_back: bfloat16 [32, 2048, 4096], P('section', 'dp'), may hold values from -0.75 to 0.75
- w_in: bfloat16 [32, 4096, 512], P('section', 'dp'), may hold values from -0.09375 to 0.09375
- w_out: bfloat16 [32, 4096, 512], P('section', 'dp'), may hold values from -0.25 to 0.25
Outputs:
- layer_out: bfloat16 [32, 2048, 4096], P('section', 'dp')
- shadow_out: bfloat16 [32, 2048, 4096], P('section', 'dp')
- input_grad: bfloat16 [32, 2048, 4096], P('section', 'dp')
- grad_w_in: float32 [32, 4096, 512], P('section', 'dp')
- grad_w_out: float32 [32, 4096, 512], P('section', 'dp')
The draws below stay inside these ranges and needn't reach their ends.
All inputs are finite; a program needn't handle non-finite values.
Results may differ from the reference program's by a relative error of at most 0.015.
Values may be sent and summed in bfloat16 or wider, within the bound.
No kernel may reach another device: no remote copies, remote signals or barrier semaphores. Data moves between devices by JAX's collectives and lax.ppermute only.
A program may use at most 128 MiB of HBM per device.

```python
import jax
import jax.numpy as jnp
from jax import lax

D = 4096
HID = 512
TOK_DEV = 256
SECTIONS = 32
TOKENS = 2048
N_DP = 8


def with_spikes(drawn, key, source, target, shards_of, factor):
    def block_of(position):
        return (jnp.arange(drawn.shape[position]) // (drawn.shape[position] // shards_of)).reshape((-1,) + (1,) * (drawn.ndim - 1 - position))

    first = jax.random.permutation(key, shards_of)[block_of(target)]
    second = (block_of(target) + shards_of // 2) % shards_of
    return jnp.where((block_of(source) == first) | (block_of(source) == second), factor * drawn, drawn)


def levels(stream_key, dims, pieces, smallest, largest):
    def one(position, blocks):
        heights = jax.random.uniform(jax.random.fold_in(jax.random.fold_in(stream_key, 6), position), (blocks,), jnp.float32, smallest / len(pieces), largest / len(pieces))
        return jnp.repeat(jnp.exp(heights), dims[position] // blocks).reshape((-1,) + (1,) * (len(dims) - position - 1))

    factor_of = one(*pieces[0])
    for cut in pieces[1:]:
        factor_of = factor_of * one(*cut)
    return factor_of


def scatter_about(key, shape, scale, reach, pieces=(), kind=jnp.bfloat16):
    level = levels(key, shape, pieces, -0.22, 0.18) if pieces else 1.0
    result = jax.random.normal(key, shape, jnp.float32) * scale * level
    return jnp.minimum(jnp.maximum(result, -reach), reach).astype(kind)


def bell_draw_with(stream_key, extent, width, reach, pieces, heavy, kind=jnp.bfloat16):
    drawn = width * jax.random.normal(stream_key, extent, jnp.float32)
    if pieces:
        drawn = drawn * levels(stream_key, extent, pieces, -0.22, 0.18)
    return jnp.clip(with_spikes(drawn, jax.random.fold_in(stream_key, 3), *heavy), -reach, reach).astype(kind)


def setup_inputs(seed: int = 0) -> dict:
    seeds = jax.random.split(jax.random.key(seed), 5)
    handoff = bell_draw_with(seeds[0], (SECTIONS, TOKENS, D), 1.0, 6.0, ((0, 32), (1, 8)), (1, 2, 8, 2.0))
    grad_back = bell_draw_with(seeds[1], (SECTIONS, TOKENS, D), 0.125, 0.75, ((0, 32), (1, 8)), (1, 2, 8, 2.0))
    w_in = scatter_about(seeds[2], (SECTIONS, D, HID), D ** -0.5, 0.09375, ((0, 32), (1, 8)))
    w_out = scatter_about(seeds[3], (SECTIONS, D, HID), HID ** -0.5, 0.25, ((0, 32), (1, 8)))
    return dict(handoff=handoff, grad_back=grad_back, w_in=w_in, w_out=w_out)


INV_ROOT_TWO = 0.7071067811865476
INV_ROOT_TWO_PI = 0.3989422804014327


def gelu_pair(preact):
    normal_cdf = 0.5 * (1.0 + lax.erf(preact * INV_ROOT_TWO))
    density = jnp.exp(-0.5 * preact * preact) * INV_ROOT_TWO_PI
    return preact * normal_cdf, normal_cdf + preact * density


def apply_layer(inputs, weight_in, weight_out):
    preact = jnp.dot(inputs, weight_in, preferred_element_type=jnp.float32)
    activated, unused_slope = gelu_pair(preact)
    hidden = activated.astype(jnp.bfloat16)
    branch = jnp.dot(hidden, weight_out.T, preferred_element_type=jnp.float32)
    output = (inputs.astype(jnp.float32) + branch).astype(jnp.bfloat16)
    return preact, hidden, output


def grouped_product(left, right):
    left_groups = left.reshape(N_DP, TOK_DEV, left.shape[1]).astype(jnp.float32)
    right_groups = right.reshape(N_DP, TOK_DEV, right.shape[1]).astype(jnp.float32)
    parts = jnp.einsum("gtd,gth->gdh", left_groups, right_groups).astype(jnp.bfloat16)
    return jnp.sum(parts, axis=0, dtype=jnp.float32)


def one_section(operands):
    inputs, upstream, weight_in, weight_out, next_in, next_out = operands
    preact, hidden, output = apply_layer(inputs, weight_in, weight_out)
    shadow = apply_layer(output, next_in, next_out)[2]
    dhidden = jnp.dot(upstream, weight_out, preferred_element_type=jnp.float32)
    unused_value, slope = gelu_pair(preact)
    dpre = (dhidden * slope).astype(jnp.bfloat16)
    back = jnp.dot(dpre, weight_in.T, preferred_element_type=jnp.float32)
    input_grad = (upstream.astype(jnp.float32) + back).astype(jnp.bfloat16)
    grad_in = grouped_product(inputs, dpre)
    grad_out = grouped_product(upstream, hidden)
    return output, shadow, input_grad, grad_in, grad_out


def reference(handoff, grad_back, w_in, w_out):
    inputs_all = jnp.roll(handoff, 1, axis=0)
    upstream_all = jnp.roll(grad_back, -1, axis=0)
    next_in_all = jnp.roll(w_in, -1, axis=0)
    next_out_all = jnp.roll(w_out, -1, axis=0)
    results = lax.map(one_section, (inputs_all, upstream_all, w_in, w_out, next_in_all, next_out_all))
    return (results[0], results[1], results[2], results[3], results[4])
```

```python
import jax
import jax.numpy as jnp
from jax import lax
from jax.experimental import pallas as pl
from jax.experimental.pallas import tpu as pltpu
from jax.sharding import PartitionSpec as P

INV_ROOT_TWO = 0.7071067811865476
INV_ROOT_TWO_PI = 0.3989422804014327
X_SIZE = 4
Y_SIZE = 2
F32 = jnp.float32
BF16 = jnp.bfloat16


def over_section(array, by):
    devices = lax.axis_size("section")
    return lax.ppermute(
        array, "section", [(i, (i + by) % devices) for i in range(devices)]
    )


def over_x(array, by):
    pairs = []
    for x in range(X_SIZE):
        for y in range(Y_SIZE):
            pairs.append((x * Y_SIZE + y, ((x + by) % X_SIZE) * Y_SIZE + y))
    return lax.ppermute(array, "dp", pairs)


def swap_y(array):
    return lax.ppermute(array, "dp", [(i, i ^ 1) for i in range(X_SIZE * Y_SIZE)])


def gelu_pair(preact):
    normal_cdf = 0.5 * (1.0 + lax.erf(preact * INV_ROOT_TWO))
    density = jnp.exp(-0.5 * preact * preact) * INV_ROOT_TWO_PI
    return (preact * normal_cdf, normal_cdf + preact * density)


def times(left, right):
    return jnp.dot(left, right, preferred_element_type=F32)


def times_transposed(left, right):
    return lax.dot_general(
        left, right, (((1,), (1,)), ((), ())), preferred_element_type=F32
    )


def weight_views(refs):
    own, partner, behind, behind_partner, ahead, ahead_partner, far_in, far_out = refs
    views = []
    for ref in (own, partner, behind, behind_partner, ahead, ahead_partner):
        half = ref.shape[0] // 2
        views.append((ref.at[pl.ds(0, half)], ref.at[pl.ds(half, half)]))
    half = far_in.shape[0] // 2
    for part in range(2):
        rows = pl.ds(part * half, half)
        views.append((far_in.at[rows], far_out.at[rows]))
    return views


def columns_of(starts, block, width):
    return pl.ds(pl.multiple_of(starts[block], width), width)


def hidden_kernel(starts, inputs, upstream, *rest):
    views, packed = weight_views(rest[:8]), rest[8]
    rows, width = views[0][0].shape
    preact = dhidden = None
    for block, (up, down) in enumerate(views):
        columns = columns_of(starts, block, rows)
        first = times(inputs[:, columns], up[...])
        second = times(upstream[:, columns], down[...])
        preact = first if preact is None else preact + first
        dhidden = second if dhidden is None else dhidden + second
    activated, slope = gelu_pair(preact)
    packed[:, :width] = activated.astype(BF16)
    packed[:, width:] = (dhidden * slope).astype(BF16)


def outputs_kernel(starts, inputs, upstream, packed, *rest):
    views, (layer_out, input_grad) = weight_views(rest[:8]), rest[8:]
    rows, width = views[0][0].shape
    for block, (up, down) in enumerate(views):
        columns = columns_of(starts, block, rows)
        branch = times_transposed(packed[:, :width], down[...])
        layer_out[:, columns] = (inputs[:, columns].astype(F32) + branch).astype(BF16)
        back = times_transposed(packed[:, width:], up[...])
        input_grad[:, columns] = (upstream[:, columns].astype(F32) + back).astype(BF16)


def shadow_kernel(starts, inputs, *rest):
    views, shadow = weight_views(rest[:8]), rest[8]
    rows, width = views[0][0].shape
    preact = None
    for block, (up, down) in enumerate(views):
        first = times(inputs[:, columns_of(starts, block, rows)], up[...])
        preact = first if preact is None else preact + first
    hidden = gelu_pair(preact)[0].astype(BF16)
    for block, (up, down) in enumerate(views):
        columns = columns_of(starts, block, rows)
        branch = times_transposed(hidden, down[...])
        shadow[:, columns] = (inputs[:, columns].astype(F32) + branch).astype(BF16)


def local_call(kernel, outs, starts, *arrays, flops):
    in_specs = [pl.BlockSpec(memory_space=pltpu.SMEM)]
    in_specs += [pl.BlockSpec(memory_space=pltpu.VMEM)] * len(arrays)
    moved = sum(a.size * a.dtype.itemsize for a in arrays)
    return pl.pallas_call(
        kernel,
        out_shape=outs,
        in_specs=in_specs,
        out_specs=jax.tree.map(lambda o: pl.BlockSpec(memory_space=pltpu.VMEM), outs),
        compiler_params=pltpu.CompilerParams(vmem_limit_bytes=40 * 2**20),
        cost_estimate=pl.CostEstimate(
            flops=flops, bytes_accessed=moved, transcendentals=0
        ),
    )(starts, *arrays)


def contract_tokens(left, right):
    return lax.dot_general(
        left, right, (((0,), (0,)), ((), ())), preferred_element_type=F32
    )


def on_device(handoff, grad_back, w_in, w_out):
    position = lax.axis_index("dp")
    x, y = position // Y_SIZE, position % Y_SIZE
    rows, width = w_in.shape[1:]
    tokens, features = handoff.shape[1:]
    starts = jnp.stack(
        [
            (lax.rem(x + by, X_SIZE) * Y_SIZE + (y + j) % Y_SIZE) * rows
            for by in (0, 3, 1, 2)
            for j in range(Y_SIZE)
        ]
    ).astype(jnp.int32)

    inputs = over_section(handoff[0], 1)
    upstream = over_section(grad_back[0], -1)
    own = jnp.concatenate([w_in[0], w_out[0]], axis=0)
    partner = swap_y(own)
    behind, ahead = over_x(own, 1), over_x(own, -1)
    behind_partner, ahead_partner = over_x(partner, 1), over_x(partner, -1)
    far_in = over_x(jnp.concatenate([behind[:rows], behind_partner[:rows]]), 1)
    far_out = over_x(jnp.concatenate([ahead[rows:], ahead_partner[rows:]]), -1)
    weights = (
        own,
        partner,
        behind,
        behind_partner,
        ahead,
        ahead_partner,
        far_in,
        far_out,
    )
    matmul = 2 * tokens * features * width

    packed = local_call(
        hidden_kernel,
        jax.ShapeDtypeStruct((tokens, 2 * width), BF16),
        starts,
        inputs,
        upstream,
        *weights,
        flops=2 * matmul,
    )
    activations = jax.ShapeDtypeStruct((tokens, features), BF16)
    layer_out, input_grad = local_call(
        outputs_kernel,
        (activations, activations),
        starts,
        inputs,
        upstream,
        packed,
        *weights,
        flops=2 * matmul,
    )
    arrived = over_section(layer_out, 1)
    shadow_back = local_call(
        shadow_kernel, activations, starts, arrived, *weights, flops=2 * matmul
    )
    shadow = over_section(shadow_back, -1)

    wide = Y_SIZE * rows
    cut = lambda array, by: lax.dynamic_slice_in_dim(
        array, lax.rem(x + by, X_SIZE) * wide, wide, axis=1
    )
    pieces, hiddens = [], [packed]
    for by in range(X_SIZE):
        piece = jnp.concatenate([cut(inputs, by), cut(upstream, by)], axis=0)
        pieces.append(piece if by == 0 else over_x(piece, by))
        if by:
            hiddens.append(over_x(packed, by))
    left_in = jnp.concatenate([p[:tokens] for p in pieces])
    left_out = jnp.concatenate([p[tokens:] for p in pieces])
    right = jnp.concatenate(hiddens)
    part = jnp.concatenate(
        [
            contract_tokens(left_in, right[:, width:]),
            contract_tokens(left_out, right[:, :width]),
        ],
        axis=1,
    )
    mine = lax.dynamic_slice_in_dim(part, y * rows, rows, axis=0)
    theirs = lax.dynamic_slice_in_dim(part, (1 - y) * rows, rows, axis=0)
    summed = mine + swap_y(theirs.astype(BF16)).astype(F32)
    return (
        layer_out[None],
        shadow[None],
        input_grad[None],
        summed[None, :, :width],
        summed[None, :, width:],
    )


def solution(mesh):
    spec = P("section", "dp", None)
    return jax.shard_map(
        on_device,
        mesh=mesh,
        in_specs=(spec,) * 4,
        out_specs=(spec,) * 5,
        check_vma=False,
    )
```

```python
import functools

import jax
import jax.numpy as jnp
from jax import lax
from jax.experimental import pallas as pl
from jax.experimental.pallas import tpu as pltpu
from jax.sharding import PartitionSpec as P

INV_ROOT_TWO = 0.7071067811865476
INV_ROOT_TWO_PI = 0.3989422804014327
X_SIZE = 4
Y_SIZE = 2
F32 = jnp.float32
BF16 = jnp.bfloat16


def over_section(array, by):
    devices = lax.axis_size("section")
    return lax.ppermute(
        array, "section", [(i, (i + by) % devices) for i in range(devices)]
    )


def over_x(array, by):
    pairs = []
    for x in range(X_SIZE):
        for y in range(Y_SIZE):
            pairs.append((x * Y_SIZE + y, ((x + by) % X_SIZE) * Y_SIZE + y))
    return lax.ppermute(array, "dp", pairs)


def swap_y(array):
    return lax.ppermute(array, "dp", [(i, i ^ 1) for i in range(X_SIZE * Y_SIZE)])


def gelu_pair(preact):
    normal_cdf = 0.5 * (1.0 + lax.erf(preact * INV_ROOT_TWO))
    density = jnp.exp(-0.5 * preact * preact) * INV_ROOT_TWO_PI
    return (preact * normal_cdf, normal_cdf + preact * density)


def times(left, right):
    return jnp.dot(left, right, preferred_element_type=F32)


def times_transposed(left, right):
    return lax.dot_general(
        left, right, (((1,), (1,)), ((), ())), preferred_element_type=F32
    )


def contract_tokens(left, right):
    return lax.dot_general(
        left, right, (((0,), (0,)), ((), ())), preferred_element_type=F32
    )


def weight_items(refs):
    near, (far_in, far_out) = refs[:6], refs[6:]
    rows = far_in.shape[0] // 2
    items = [((ref, 0), (ref, rows)) for ref in near]
    items += [((far_in, part * rows), (far_out, part * rows)) for part in range(2)]
    return rows, items


def columns_of(starts, block, width):
    return pl.ds(pl.multiple_of(starts[block], width), width)


class Loads:
    def __init__(self, semaphores):
        self.semaphores, self.copies, self.waited = semaphores, [], set()

    def start(self, source, target):
        number = len(self.copies)
        copy = pltpu.make_async_copy(source, target, self.semaphores.at[number])
        copy.start()
        self.copies.append((copy, target))
        return number

    def get(self, number):
        copy, target = self.copies[number]
        if number not in self.waited:
            self.waited.add(number)
            copy.wait()
        return target

    def finish(self):
        for number in range(len(self.copies)):
            self.get(number)


def hidden_kernel(starts, inputs, upstream, *rest):
    (rows, items), rest = weight_items(rest[:8]), rest[8:]
    hidden, dpre, left, right, up, down, semaphores = rest
    loads, numbers = Loads(semaphores), []
    for block, ((up_ref, up_row), (down_ref, down_row)) in enumerate(items):
        columns = columns_of(starts, block, rows)
        numbers.append(
            (
                loads.start(inputs.at[:, columns], left.at[block]),
                loads.start(up_ref.at[pl.ds(up_row, rows)], up.at[block]),
                loads.start(upstream.at[:, columns], right.at[block]),
                loads.start(down_ref.at[pl.ds(down_row, rows)], down.at[block]),
            )
        )
    preact = dhidden = None
    for one, two, three, four in numbers:
        first = times(loads.get(one)[...], loads.get(two)[...])
        second = times(loads.get(three)[...], loads.get(four)[...])
        preact = first if preact is None else preact + first
        dhidden = second if dhidden is None else dhidden + second
    activated, slope = gelu_pair(preact)
    hidden[...] = activated.astype(BF16)
    dpre[...] = (dhidden * slope).astype(BF16)


def residual_kernel(which, starts, inputs, inner, *rest):
    (rows, items), rest = weight_items(rest[:8]), rest[8:]
    output, left, weight, result, semaphores = rest
    loads, numbers = Loads(semaphores), []
    for block, item in enumerate(items):
        ref, row = item[which]
        numbers.append(
            (
                loads.start(ref.at[pl.ds(row, rows)], weight.at[block]),
                loads.start(
                    inputs.at[:, columns_of(starts, block, rows)], left.at[block]
                ),
            )
        )
    for block, (one, two) in enumerate(numbers):
        branch = times_transposed(inner[...], loads.get(one)[...])
        total = loads.get(two)[...].astype(F32) + branch
        result[block] = total.astype(BF16)
        loads.start(
            result.at[block], output.at[:, columns_of(starts, block, rows)]
        )
    loads.finish()


def shadow_kernel(starts, inputs, *rest):
    (rows, items), rest = weight_items(rest[:8]), rest[8:]
    output, left, up, down, result, semaphores = rest
    loads, numbers = Loads(semaphores), []
    for block, ((ref, row), _) in enumerate(items):
        columns = columns_of(starts, block, rows)
        numbers.append(
            (
                loads.start(inputs.at[:, columns], left.at[block]),
                loads.start(ref.at[pl.ds(row, rows)], up.at[block]),
            )
        )
    downs = []
    for block, (_, (ref, row)) in enumerate(items):
        downs.append(loads.start(ref.at[pl.ds(row, rows)], down.at[block]))
    preact = None
    for one, two in numbers:
        first = times(loads.get(one)[...], loads.get(two)[...])
        preact = first if preact is None else preact + first
    hidden = gelu_pair(preact)[0].astype(BF16)
    for block, number in enumerate(downs):
        branch = times_transposed(hidden, loads.get(number)[...])
        total = left[block].astype(F32) + branch
        result[block] = total.astype(BF16)
        loads.start(
            result.at[block], output.at[:, columns_of(starts, block, rows)]
        )
    loads.finish()


def part_kernel(starts, whole, other, *rest):
    pieces, (part, lefts, rights, semaphores) = rest[:-4], rest[-4:]
    rows, width = part.shape
    count = lefts.shape[0] - 1
    joined = len(pieces) == count
    loads, numbers = Loads(semaphores), []
    numbers.append(
        (
            loads.start(whole.at[:, columns_of(starts, 0, rows)], lefts.at[0]),
            loads.start(other, rights.at[0]),
        )
    )
    for k in range(count):
        piece = pieces[k]
        if joined:
            right = piece.at[:, pl.ds(piece.shape[1] - width, width)]
        else:
            right = pieces[count + k]
        numbers.append(
            (
                loads.start(
                    piece.at[:, columns_of(starts, 1, rows)], lefts.at[k + 1]
                ),
                loads.start(right, rights.at[k + 1]),
            )
        )
    total = None
    for one, two in numbers:
        product = contract_tokens(loads.get(one)[...], loads.get(two)[...])
        total = product if total is None else total + product
    part[...] = total.astype(part.dtype)


def copy_kernel(source, target, semaphores):
    loads, count = Loads(semaphores), semaphores.shape[0]
    rows = source.shape[0] // count
    for k in range(count):
        some = pl.ds(k * rows, rows)
        loads.start(source.at[some], target.at[some])
    loads.finish()


ANY = pl.BlockSpec(memory_space=pl.ANY)
VMEM = pl.BlockSpec(memory_space=pltpu.VMEM)
SMEM = pl.BlockSpec(memory_space=pltpu.SMEM)


def local_call(kernel, outs, in_specs, out_specs, scratch, copies, *arrays):
    return pl.pallas_call(
        kernel,
        out_shape=outs,
        in_specs=in_specs,
        out_specs=out_specs,
        scratch_shapes=[*scratch, pltpu.SemaphoreType.DMA((copies,))],
        compiler_params=pltpu.CompilerParams(vmem_limit_bytes=56 * 2**20),
        cost_estimate=pl.CostEstimate(flops=1, bytes_accessed=1, transcendentals=0),
    )(*arrays)


def on_device(handoff, grad_back, w_in, w_out):
    position = lax.axis_index("dp")
    x, y = position // Y_SIZE, position % Y_SIZE
    rows, width = w_in.shape[1:]
    tokens, features = handoff.shape[1:]
    starts = jnp.stack(
        [
            (lax.rem(x + by, X_SIZE) * Y_SIZE + (y + j) % Y_SIZE) * rows
            for by in (0, 3, 1, 2)
            for j in range(Y_SIZE)
        ]
    ).astype(jnp.int32)

    own = jnp.concatenate([w_in[0], w_out[0]], axis=0)
    partner = swap_y(own)
    behind, ahead = over_x(own, 1), over_x(own, -1)
    handoff, grad_back, partner = lax.optimization_barrier(
        (handoff, grad_back, partner)
    )
    behind_partner, ahead_partner = over_x(partner, 1), over_x(partner, -1)
    inputs = over_section(handoff[0], 1)
    upstream = over_section(grad_back[0], -1)
    far_in = over_x(jnp.concatenate([behind[:rows], behind_partner[:rows]]), 1)
    far_out = over_x(jnp.concatenate([ahead[rows:], ahead_partner[rows:]]), -1)
    weights = (
        own,
        partner,
        behind,
        behind_partner,
        ahead,
        ahead_partner,
        far_in,
        far_out,
    )
    blocks = X_SIZE * Y_SIZE
    activations = jax.ShapeDtypeStruct((tokens, features), BF16)
    half = jax.ShapeDtypeStruct((tokens, width), BF16)
    token_blocks = pltpu.VMEM((blocks, tokens, rows), BF16)
    weight_blocks = pltpu.VMEM((blocks, rows, width), BF16)
    wide = Y_SIZE * rows

    def cut(array, by):
        first = lax.rem(x + by, X_SIZE) * wide
        return lax.dynamic_slice_in_dim(array, first, wide, axis=1)

    inputs_out = [cut(inputs, by) for by in range(1, X_SIZE)]
    inputs_pieces = [over_x(p, by + 1) for by, p in enumerate(inputs_out)]
    first_starts, _ = lax.optimization_barrier((starts, inputs_out))

    hidden, dpre = local_call(
        hidden_kernel,
        (half, half),
        [SMEM] + [ANY] * 10,
        (VMEM, VMEM),
        [token_blocks, token_blocks, weight_blocks, weight_blocks],
        4 * blocks,
        first_starts,
        inputs,
        upstream,
        *weights,
    )

    def residual(which, base, inner):
        return local_call(
            functools.partial(residual_kernel, which),
            activations,
            [SMEM, ANY, VMEM] + [ANY] * 8,
            ANY,
            [token_blocks, weight_blocks, token_blocks],
            3 * blocks,
            starts,
            base,
            inner,
            *weights,
        )

    layer_out = residual(1, inputs, hidden)
    arrived = over_section(layer_out, 1)
    input_grad = residual(0, upstream, dpre)

    dpre_pieces = [over_x(dpre, by) for by in range(1, X_SIZE)]
    joint_pieces = [
        over_x(jnp.concatenate([cut(upstream, by), hidden], axis=1), by)
        for by in range(1, X_SIZE)
    ]
    ours = jnp.stack([x * wide + y * rows, y * rows]).astype(jnp.int32)
    other = jnp.stack([x * wide + (1 - y) * rows, (1 - y) * rows]).astype(jnp.int32)

    def part(where, kind, *arrays):
        return local_call(
            part_kernel,
            jax.ShapeDtypeStruct((rows, width), kind),
            [SMEM] + [ANY] * len(arrays),
            VMEM,
            [
                pltpu.VMEM((X_SIZE, tokens, rows), BF16),
                pltpu.VMEM((X_SIZE, tokens, width), BF16),
            ],
            2 * X_SIZE,
            where,
            *arrays,
        )

    arrays = (inputs, dpre, *inputs_pieces, *dpre_pieces)
    theirs_in = part(other, BF16, *arrays)
    mine_in = part(ours, F32, *arrays)
    received_in = swap_y(theirs_in)

    arrived, input_grad, mine_in = lax.optimization_barrier(
        (arrived, input_grad, mine_in)
    )
    shadow_back = local_call(
        shadow_kernel,
        activations,
        [SMEM] + [ANY] * 9,
        ANY,
        [token_blocks, weight_blocks, weight_blocks, token_blocks],
        4 * blocks,
        starts,
        arrived,
        *weights,
    )
    shadow = over_section(shadow_back, -1)

    arrays = (upstream, hidden, *joint_pieces)
    theirs_out = part(other, BF16, *arrays)
    mine_out = part(ours, F32, *arrays)
    received_out = swap_y(theirs_out)
    grad_in = mine_in + received_in.astype(F32)
    shadow = local_call(copy_kernel, activations, [ANY], ANY, [], 8, shadow)
    shadow, received_out, grad_in = lax.optimization_barrier(
        (shadow, received_out, grad_in)
    )
    grad_out = mine_out + received_out.astype(F32)
    return (
        layer_out[None],
        shadow[None],
        input_grad[None],
        grad_in[None],
        grad_out[None],
    )


def solution(mesh):
    spec = P("section", "dp", None)
    return jax.shard_map(
        on_device,
        mesh=mesh,
        in_specs=(spec,) * 4,
        out_specs=(spec,) * 5,
        check_vma=False,
    )
```

```python
import jax
import jax.numpy as jnp
from jax import lax
from jax.experimental import pallas as pl
from jax.experimental.pallas import tpu as pltpu
from jax.sharding import PartitionSpec as P

INV_ROOT_TWO = 0.7071067811865476
INV_ROOT_TWO_PI = 0.3989422804014327
X_SIZE = 4
Y_SIZE = 2
F32 = jnp.float32
BF16 = jnp.bfloat16


def over_section(array, by):
    devices = lax.axis_size("section")
    return lax.ppermute(
        array, "section", [(i, (i + by) % devices) for i in range(devices)]
    )


def over_x(array, by):
    pairs = []
    for x in range(X_SIZE):
        for y in range(Y_SIZE):
            pairs.append((x * Y_SIZE + y, ((x + by) % X_SIZE) * Y_SIZE + y))
    return lax.ppermute(array, "dp", pairs)


def swap_y(array):
    return lax.ppermute(array, "dp", [(i, i ^ 1) for i in range(X_SIZE * Y_SIZE)])


def gelu_pair(preact):
    normal_cdf = 0.5 * (1.0 + lax.erf(preact * INV_ROOT_TWO))
    density = jnp.exp(-0.5 * preact * preact) * INV_ROOT_TWO_PI
    return (preact * normal_cdf, normal_cdf + preact * density)


def times(left, right):
    return jnp.dot(left, right, preferred_element_type=F32)


def times_transposed(left, right):
    return lax.dot_general(
        left, right, (((1,), (1,)), ((), ())), preferred_element_type=F32
    )


def contract_tokens(left, right):
    return lax.dot_general(
        left, right, (((0,), (0,)), ((), ())), preferred_element_type=F32
    )


def weight_items(refs):
    near, far = refs[:6], refs[6:]
    rows = far[0].shape[0]
    items = [((ref, 0), (ref, rows)) for ref in near]
    items += [((far[k], 0), (far[k + 1], 0)) for k in range(0, len(far), 2)]
    return rows, items


def columns_of(starts, block, width):
    return pl.ds(pl.multiple_of(starts[block], width), width)


class Loads:
    def __init__(self, semaphores):
        self.semaphores, self.copies, self.waited = semaphores, [], set()

    def start(self, source, target):
        number = len(self.copies)
        copy = pltpu.make_async_copy(source, target, self.semaphores.at[number])
        copy.start()
        self.copies.append((copy, target))
        return number

    def get(self, number):
        copy, target = self.copies[number]
        if number not in self.waited:
            self.waited.add(number)
            copy.wait()
        return target

    def finish(self):
        for number in range(len(self.copies)):
            self.get(number)


def first_kernel(starts, inputs, *rest):
    (rows, items), rest = weight_items(rest[:8]), rest[8:]
    partial, left, up, semaphores = rest
    loads, numbers = Loads(semaphores), []
    for block, ((ref, row), _) in enumerate(items):
        columns = columns_of(starts, block, rows)
        numbers.append(
            (
                loads.start(inputs.at[:, columns], left.at[block]),
                loads.start(ref.at[pl.ds(row, rows)], up.at[block]),
            )
        )
    total = None
    for one, two in numbers:
        product = times(loads.get(one)[...], loads.get(two)[...])
        total = product if total is None else total + product
    partial[...] = total


def layer_kernel(starts, inputs, partial, *rest):
    (rows, items), rest = weight_items(rest[:10]), rest[10:]
    hidden, slope, output, left, up, down, result, semaphores = rest
    loads, lefts, downs = Loads(semaphores), [], []
    last = len(items) - 1
    order = [last, *range(last)]
    ref, row = items[last][0]
    up_number = loads.start(ref.at[pl.ds(row, rows)], up)
    for block in order:
        columns = columns_of(starts, block, rows)
        lefts.append(loads.start(inputs.at[:, columns], left.at[block]))
        ref, row = items[block][1]
        downs.append(loads.start(ref.at[pl.ds(row, rows)], down.at[block]))
    product = times(loads.get(lefts[0])[...], loads.get(up_number)[...])
    activated, gradient = gelu_pair(partial[...] + product)
    inner = activated.astype(BF16)
    hidden[...] = inner
    slope[...] = gradient
    for block, one, two in zip(order, lefts, downs):
        branch = times_transposed(inner, loads.get(two)[...])
        total = loads.get(one)[...].astype(F32) + branch
        result[block] = total.astype(BF16)
        loads.start(
            result.at[block], output.at[:, columns_of(starts, block, rows)]
        )
    loads.finish()


def back_kernel(starts, upstream, slope, *rest):
    (rows, items), rest = weight_items(rest[:10]), rest[10:]
    dpre, output, left, up, down, result, semaphores = rest
    loads, numbers, ups = Loads(semaphores), [], []
    for block, (_, (ref, row)) in enumerate(items):
        columns = columns_of(starts, block, rows)
        numbers.append(
            (
                loads.start(upstream.at[:, columns], left.at[block]),
                loads.start(ref.at[pl.ds(row, rows)], down.at[block]),
            )
        )
    for block, ((ref, row), _) in enumerate(items):
        ups.append(loads.start(ref.at[pl.ds(row, rows)], up.at[block]))
    dhidden = None
    for one, two in numbers:
        product = times(loads.get(one)[...], loads.get(two)[...])
        dhidden = product if dhidden is None else dhidden + product
    inner = (dhidden * slope[...]).astype(BF16)
    dpre[...] = inner
    for block, number in enumerate(ups):
        back = times_transposed(inner, loads.get(number)[...])
        total = left[block].astype(F32) + back
        result[block] = total.astype(BF16)
        loads.start(
            result.at[block], output.at[:, columns_of(starts, block, rows)]
        )
    loads.finish()


def shadow_kernel(starts, inputs, *rest):
    (rows, items), rest = weight_items(rest[:10]), rest[10:]
    output, left, up, down, result, semaphores = rest
    loads, numbers = Loads(semaphores), []
    for block, ((ref, row), _) in enumerate(items):
        columns = columns_of(starts, block, rows)
        numbers.append(
            (
                loads.start(inputs.at[:, columns], left.at[block]),
                loads.start(ref.at[pl.ds(row, rows)], up.at[block]),
            )
        )
    downs = []
    for block, (_, (ref, row)) in enumerate(items):
        downs.append(loads.start(ref.at[pl.ds(row, rows)], down.at[block]))
    preact = None
    for one, two in numbers:
        first = times(loads.get(one)[...], loads.get(two)[...])
        preact = first if preact is None else preact + first
    hidden = gelu_pair(preact)[0].astype(BF16)
    for block, number in enumerate(downs):
        branch = times_transposed(hidden, loads.get(number)[...])
        total = left[block].astype(F32) + branch
        result[block] = total.astype(BF16)
        loads.start(
            result.at[block], output.at[:, columns_of(starts, block, rows)]
        )
    loads.finish()


def part_kernel(starts, whole, other, *rest):
    pieces, (part, lefts, rights, semaphores) = rest[:-4], rest[-4:]
    rows, width = part.shape
    loads, numbers = Loads(semaphores), []
    numbers.append(
        (
            loads.start(whole.at[:, columns_of(starts, 0, rows)], lefts.at[0]),
            loads.start(other, rights.at[0]),
        )
    )
    for k, piece in enumerate(pieces):
        right = piece.at[:, pl.ds(piece.shape[1] - width, width)]
        numbers.append(
            (
                loads.start(
                    piece.at[:, columns_of(starts, 1, rows)], lefts.at[k + 1]
                ),
                loads.start(right, rights.at[k + 1]),
            )
        )
    total = None
    for one, two in numbers:
        product = contract_tokens(loads.get(one)[...], loads.get(two)[...])
        total = product if total is None else total + product
    part[...] = total.astype(part.dtype)


def copy_kernel(source, target, held, semaphores):
    loads, count = Loads(semaphores), semaphores.shape[0] // 2
    rows = source.shape[0] // count
    for k in range(count):
        some = pl.ds(k * rows, rows)
        loads.start(source.at[some], held.at[some])
    for k in range(count):
        some = pl.ds(k * rows, rows)
        loads.get(k)
        loads.start(held.at[some], target.at[some])
    loads.finish()


ANY = pl.BlockSpec(memory_space=pl.ANY)
VMEM = pl.BlockSpec(memory_space=pltpu.VMEM)
SMEM = pl.BlockSpec(memory_space=pltpu.SMEM)


def local_call(kernel, outs, in_specs, out_specs, scratch, copies, *arrays):
    return pl.pallas_call(
        kernel,
        out_shape=outs,
        in_specs=in_specs,
        out_specs=out_specs,
        scratch_shapes=[*scratch, pltpu.SemaphoreType.DMA((copies,))],
        compiler_params=pltpu.CompilerParams(vmem_limit_bytes=56 * 2**20),
        cost_estimate=pl.CostEstimate(flops=1, bytes_accessed=1, transcendentals=0),
    )(*arrays)


def on_device(handoff, grad_back, w_in, w_out):
    position = lax.axis_index("dp")
    x, y = position // Y_SIZE, position % Y_SIZE
    rows, width = w_in.shape[1:]
    tokens, features = handoff.shape[1:]
    places = ((0, 0), (0, 1), (3, 0), (1, 0), (3, 1), (1, 1), (2, 0), (2, 1))
    starts = jnp.stack(
        [(lax.rem(x + i, X_SIZE) * Y_SIZE + (y + j) % Y_SIZE) * rows for i, j in places]
    ).astype(jnp.int32)

    own = jnp.concatenate([w_in[0], w_out[0]], axis=0)
    partner = swap_y(own)
    behind, ahead = over_x(own, 1), over_x(own, -1)
    handoff, partner, behind, ahead = lax.optimization_barrier(
        (handoff, partner, behind, ahead)
    )
    behind_partner, ahead_partner = over_x(partner, 1), over_x(partner, -1)
    far_in, far_out = over_x(behind[:rows], 1), over_x(ahead[rows:], -1)
    inputs = over_section(handoff[0], 1)
    far_partner_in = over_x(behind_partner[:rows], 1)
    far_partner_out = over_x(ahead_partner[rows:], -1)
    grad_back, inputs = lax.optimization_barrier((grad_back, inputs))
    upstream = over_section(grad_back[0], -1)
    weights = (own, partner, behind, ahead, behind_partner, ahead_partner)
    weights += (far_in, far_out, far_partner_in, far_partner_out)

    blocks = X_SIZE * Y_SIZE
    activations = jax.ShapeDtypeStruct((tokens, features), BF16)
    half = jax.ShapeDtypeStruct((tokens, width), BF16)
    half_wide = jax.ShapeDtypeStruct((tokens, width), F32)
    token_blocks = pltpu.VMEM((blocks, tokens, rows), BF16)
    weight_blocks = pltpu.VMEM((blocks, rows, width), BF16)
    any_weights = [ANY] * len(weights)
    wide = Y_SIZE * rows

    def cut(array, by):
        first = lax.rem(x + by, X_SIZE) * wide
        return lax.dynamic_slice_in_dim(array, first, wide, axis=1)

    partial = local_call(
        first_kernel,
        half_wide,
        [SMEM, ANY] + [ANY] * 8,
        VMEM,
        [token_blocks, weight_blocks],
        2 * blocks,
        starts,
        inputs,
        *weights[:8],
    )
    hidden, slope, layer_out = local_call(
        layer_kernel,
        (half, half_wide, activations),
        [SMEM, ANY, VMEM] + any_weights,
        (VMEM, VMEM, ANY),
        [token_blocks, pltpu.VMEM((rows, width), BF16), weight_blocks, token_blocks],
        3 * blocks + 1,
        starts,
        inputs,
        partial,
        *weights,
    )
    arrived = over_section(layer_out, 1)
    out_pieces = [
        over_x(jnp.concatenate([cut(upstream, by), hidden], axis=1), by)
        for by in range(1, X_SIZE)
    ]
    dpre, input_grad = local_call(
        back_kernel,
        (half, activations),
        [SMEM, ANY, VMEM] + any_weights,
        (VMEM, ANY),
        [token_blocks, weight_blocks, weight_blocks, token_blocks],
        4 * blocks,
        starts,
        upstream,
        slope,
        *weights,
    )
    arrived, input_grad = lax.optimization_barrier((arrived, input_grad))
    shadow_back = local_call(
        shadow_kernel,
        activations,
        [SMEM, ANY] + any_weights,
        ANY,
        [token_blocks, weight_blocks, weight_blocks, token_blocks],
        4 * blocks,
        starts,
        arrived,
        *weights,
    )
    shadow = over_section(shadow_back, -1)

    in_pieces = [
        jnp.concatenate([cut(inputs, by), dpre], axis=1) for by in range(1, X_SIZE)
    ]
    in_pieces, out_pieces, shadow_back = lax.optimization_barrier(
        (in_pieces, out_pieces, shadow_back)
    )
    in_pieces = [over_x(piece, by + 1) for by, piece in enumerate(in_pieces)]
    ours = jnp.stack([x * wide + y * rows, y * rows]).astype(jnp.int32)
    apart = (1 - y) * rows
    other = jnp.stack([x * wide + apart, apart]).astype(jnp.int32)

    def part(where, kind, *arrays):
        return local_call(
            part_kernel,
            jax.ShapeDtypeStruct((rows, width), kind),
            [SMEM] + [ANY] * len(arrays),
            VMEM,
            [
                pltpu.VMEM((X_SIZE, tokens, rows), BF16),
                pltpu.VMEM((X_SIZE, tokens, width), BF16),
            ],
            2 * X_SIZE,
            where,
            *arrays,
        )

    received_out = swap_y(part(other, BF16, upstream, hidden, *out_pieces))
    mine_out = part(ours, F32, upstream, hidden, *out_pieces)
    received_in = swap_y(part(other, BF16, inputs, dpre, *in_pieces))
    mine_in = part(ours, F32, inputs, dpre, *in_pieces)
    grad_out = mine_out + received_out.astype(F32)
    shadow = local_call(
        copy_kernel,
        activations,
        [ANY],
        ANY,
        [pltpu.VMEM((tokens, features), BF16)],
        16,
        shadow,
    )
    shadow, received_in, grad_out = lax.optimization_barrier(
        (shadow, received_in, grad_out)
    )
    grad_in = mine_in + received_in.astype(F32)
    return (
        layer_out[None],
        shadow[None],
        input_grad[None],
        grad_in[None],
        grad_out[None],
    )


def solution(mesh):
    spec = P("section", "dp", None)
    return jax.shard_map(
        on_device,
        mesh=mesh,
        in_specs=(spec,) * 4,
        out_specs=(spec,) * 5,
        check_vma=False,
    )
```

```python
import jax
import jax.numpy as jnp
from jax import lax
from jax.experimental import pallas as pl
from jax.experimental.pallas import tpu as pltpu
from jax.sharding import PartitionSpec as P

INV_ROOT_TWO = 0.7071067811865476
INV_ROOT_TWO_PI = 0.3989422804014327
X_SIZE = 4
Y_SIZE = 2
F32 = jnp.float32
BF16 = jnp.bfloat16


def over_section(array, by):
    devices = lax.axis_size("section")
    return lax.ppermute(
        array, "section", [(i, (i + by) % devices) for i in range(devices)]
    )


def over_x(array, by):
    pairs = []
    for x in range(X_SIZE):
        for y in range(Y_SIZE):
            pairs.append((x * Y_SIZE + y, ((x + by) % X_SIZE) * Y_SIZE + y))
    return lax.ppermute(array, "dp", pairs)


def swap_y(array):
    return lax.ppermute(array, "dp", [(i, i ^ 1) for i in range(X_SIZE * Y_SIZE)])


def gelu_pair(preact):
    normal_cdf = 0.5 * (1.0 + lax.erf(preact * INV_ROOT_TWO))
    density = jnp.exp(-0.5 * preact * preact) * INV_ROOT_TWO_PI
    return (preact * normal_cdf, normal_cdf + preact * density)


def times(left, right):
    return jnp.dot(left, right, preferred_element_type=F32)


def times_transposed(left, right):
    return lax.dot_general(
        left, right, (((1,), (1,)), ((), ())), preferred_element_type=F32
    )


def contract_tokens(left, right):
    return lax.dot_general(
        left, right, (((0,), (0,)), ((), ())), preferred_element_type=F32
    )


def weight_items(refs):
    near, far = refs[:6], refs[6:]
    rows = far[0].shape[0]
    items = [((ref, 0), (ref, rows)) for ref in near]
    items += [((far[k], 0), (far[k + 1], 0)) for k in range(0, len(far), 2)]
    return rows, items


def columns_of(starts, block, width):
    return pl.ds(pl.multiple_of(starts[block], width), width)


class Loads:
    def __init__(self, semaphores):
        self.semaphores, self.copies, self.waited = semaphores, [], set()

    def start(self, source, target):
        number = len(self.copies)
        copy = pltpu.make_async_copy(source, target, self.semaphores.at[number])
        copy.start()
        self.copies.append((copy, target))
        return number

    def get(self, number):
        copy, target = self.copies[number]
        if number not in self.waited:
            self.waited.add(number)
            copy.wait()
        return target

    def finish(self):
        for number in range(len(self.copies)):
            self.get(number)


def first_kernel(starts, inputs, *rest):
    (rows, items), rest = weight_items(rest[:8]), rest[8:]
    partial, left, up, semaphores = rest
    loads, numbers = Loads(semaphores), []
    for block, ((ref, row), _) in enumerate(items):
        columns = columns_of(starts, block, rows)
        numbers.append(
            (
                loads.start(inputs.at[:, columns], left.at[block]),
                loads.start(ref.at[pl.ds(row, rows)], up.at[block]),
            )
        )
    total = None
    for one, two in numbers:
        product = times(loads.get(one)[...], loads.get(two)[...])
        total = product if total is None else total + product
    partial[...] = total


def layer_kernel(starts, inputs, partial, *rest):
    (rows, items), rest = weight_items(rest[:10]), rest[10:]
    hidden, slope, output, left, up, down, result, semaphores = rest
    loads, lefts, downs = Loads(semaphores), [], []
    last = len(items) - 1
    order = [last, *range(last)]
    ref, row = items[last][0]
    up_number = loads.start(ref.at[pl.ds(row, rows)], up)
    for block in order:
        columns = columns_of(starts, block, rows)
        lefts.append(loads.start(inputs.at[:, columns], left.at[block]))
        ref, row = items[block][1]
        downs.append(loads.start(ref.at[pl.ds(row, rows)], down.at[block]))
    product = times(loads.get(lefts[0])[...], loads.get(up_number)[...])
    activated, gradient = gelu_pair(partial[...] + product)
    inner = activated.astype(BF16)
    hidden[...] = inner
    slope[...] = gradient
    for block, one, two in zip(order, lefts, downs):
        branch = times_transposed(inner, loads.get(two)[...])
        total = loads.get(one)[...].astype(F32) + branch
        result[block] = total.astype(BF16)
        loads.start(
            result.at[block], output.at[:, columns_of(starts, block, rows)]
        )
    loads.finish()


def back_kernel(starts, upstream, slope, *rest):
    (rows, items), rest = weight_items(rest[:10]), rest[10:]
    dpre, output, left, up, down, result, semaphores = rest
    loads, numbers, ups = Loads(semaphores), [], []
    for block, (_, (ref, row)) in enumerate(items):
        columns = columns_of(starts, block, rows)
        numbers.append(
            (
                loads.start(upstream.at[:, columns], left.at[block]),
                loads.start(ref.at[pl.ds(row, rows)], down.at[block]),
            )
        )
    for block, ((ref, row), _) in enumerate(items):
        ups.append(loads.start(ref.at[pl.ds(row, rows)], up.at[block]))
    dhidden = None
    for one, two in numbers:
        product = times(loads.get(one)[...], loads.get(two)[...])
        dhidden = product if dhidden is None else dhidden + product
    inner = (dhidden * slope[...]).astype(BF16)
    dpre[...] = inner
    for block, number in enumerate(ups):
        back = times_transposed(inner, loads.get(number)[...])
        total = left[block].astype(F32) + back
        result[block] = total.astype(BF16)
        loads.start(
            result.at[block], output.at[:, columns_of(starts, block, rows)]
        )
    loads.finish()


def shadow_kernel(starts, inputs, *rest):
    (rows, items), rest = weight_items(rest[:10]), rest[10:]
    output, left, up, down, result, semaphores = rest
    loads, numbers = Loads(semaphores), []
    for block, ((ref, row), _) in enumerate(items):
        columns = columns_of(starts, block, rows)
        numbers.append(
            (
                loads.start(inputs.at[:, columns], left.at[block]),
                loads.start(ref.at[pl.ds(row, rows)], up.at[block]),
            )
        )
    downs = []
    for block, (_, (ref, row)) in enumerate(items):
        downs.append(loads.start(ref.at[pl.ds(row, rows)], down.at[block]))
    preact = None
    for one, two in numbers:
        first = times(loads.get(one)[...], loads.get(two)[...])
        preact = first if preact is None else preact + first
    hidden = gelu_pair(preact)[0].astype(BF16)
    for block, number in enumerate(downs):
        branch = times_transposed(hidden, loads.get(number)[...])
        total = left[block].astype(F32) + branch
        result[block] = total.astype(BF16)
        loads.start(
            result.at[block], output.at[:, columns_of(starts, block, rows)]
        )
    loads.finish()


def part_kernel(starts, whole, other, *rest):
    pieces, (part, lefts, rights, semaphores) = rest[:-4], rest[-4:]
    rows, width = part.shape
    loads, numbers = Loads(semaphores), []
    numbers.append(
        (
            loads.start(whole.at[:, columns_of(starts, 0, rows)], lefts.at[0]),
            loads.start(other, rights.at[0]),
        )
    )
    count = len(pieces) // 2
    for k, (left, right) in enumerate(zip(pieces[:count], pieces[count:])):
        right = right.at[:, pl.ds(right.shape[1] - width, width)]
        numbers.append(
            (
                loads.start(
                    left.at[:, columns_of(starts, 1, rows)], lefts.at[k + 1]
                ),
                loads.start(right, rights.at[k + 1]),
            )
        )
    total = None
    for one, two in numbers:
        product = contract_tokens(loads.get(one)[...], loads.get(two)[...])
        total = product if total is None else total + product
    part[...] = total.astype(part.dtype)


def copy_kernel(source, target, held, semaphores):
    loads, count = Loads(semaphores), semaphores.shape[0] // 2
    rows = source.shape[0] // count
    for k in range(count):
        some = pl.ds(k * rows, rows)
        loads.start(source.at[some], held.at[some])
    for k in range(count):
        some = pl.ds(k * rows, rows)
        loads.get(k)
        loads.start(held.at[some], target.at[some])
    loads.finish()


ANY = pl.BlockSpec(memory_space=pl.ANY)
VMEM = pl.BlockSpec(memory_space=pltpu.VMEM)
SMEM = pl.BlockSpec(memory_space=pltpu.SMEM)


def local_call(kernel, outs, in_specs, out_specs, scratch, copies, *arrays):
    return pl.pallas_call(
        kernel,
        out_shape=outs,
        in_specs=in_specs,
        out_specs=out_specs,
        scratch_shapes=[*scratch, pltpu.SemaphoreType.DMA((copies,))],
        compiler_params=pltpu.CompilerParams(vmem_limit_bytes=56 * 2**20),
        cost_estimate=pl.CostEstimate(flops=1, bytes_accessed=1, transcendentals=0),
    )(*arrays)


def on_device(handoff, grad_back, w_in, w_out):
    position = lax.axis_index("dp")
    x, y = position // Y_SIZE, position % Y_SIZE
    rows, width = w_in.shape[1:]
    tokens, features = handoff.shape[1:]
    places = ((0, 0), (0, 1), (3, 0), (1, 0), (3, 1), (1, 1), (2, 0), (2, 1))
    starts = jnp.stack(
        [(lax.rem(x + i, X_SIZE) * Y_SIZE + (y + j) % Y_SIZE) * rows for i, j in places]
    ).astype(jnp.int32)

    own = jnp.concatenate([w_in[0], w_out[0]], axis=0)
    partner = swap_y(own)
    behind, ahead = over_x(own, 1), over_x(own, -1)
    handoff, partner, behind, ahead = lax.optimization_barrier(
        (handoff, partner, behind, ahead)
    )
    behind_partner, ahead_partner = over_x(partner, 1), over_x(partner, -1)
    far_in, far_out = over_x(behind[:rows], 1), over_x(ahead[rows:], -1)
    inputs = over_section(handoff[0], 1)
    far_partner_in = over_x(behind_partner[:rows], 1)
    far_partner_out = over_x(ahead_partner[rows:], -1)
    grad_back, inputs = lax.optimization_barrier((grad_back, inputs))
    upstream = over_section(grad_back[0], -1)
    weights = (own, partner, behind, ahead, behind_partner, ahead_partner)
    weights += (far_in, far_out, far_partner_in, far_partner_out)

    blocks = X_SIZE * Y_SIZE
    activations = jax.ShapeDtypeStruct((tokens, features), BF16)
    half = jax.ShapeDtypeStruct((tokens, width), BF16)
    half_wide = jax.ShapeDtypeStruct((tokens, width), F32)
    token_blocks = pltpu.VMEM((blocks, tokens, rows), BF16)
    weight_blocks = pltpu.VMEM((blocks, rows, width), BF16)
    any_weights = [ANY] * len(weights)
    wide = Y_SIZE * rows

    def cut(array, by):
        first = lax.rem(x + by, X_SIZE) * wide
        return lax.dynamic_slice_in_dim(array, first, wide, axis=1)

    partial = local_call(
        first_kernel,
        half_wide,
        [SMEM, ANY] + [ANY] * 8,
        VMEM,
        [token_blocks, weight_blocks],
        2 * blocks,
        starts,
        inputs,
        *weights[:8],
    )
    hidden, slope, layer_out = local_call(
        layer_kernel,
        (half, half_wide, activations),
        [SMEM, ANY, VMEM] + any_weights,
        (VMEM, VMEM, ANY),
        [token_blocks, pltpu.VMEM((rows, width), BF16), weight_blocks, token_blocks],
        3 * blocks + 1,
        starts,
        inputs,
        partial,
        *weights,
    )
    steps = range(1, X_SIZE)
    opposite = X_SIZE // 2
    near_inputs = {by: over_x(cut(inputs, by), by) for by in steps if by != opposite}
    ready, near_inputs = lax.optimization_barrier((layer_out, near_inputs))
    arrived = over_section(ready, 1)
    out_pieces = [
        over_x(jnp.concatenate([cut(upstream, by), hidden], axis=1), by)
        for by in range(1, X_SIZE)
    ]
    dpre, input_grad = local_call(
        back_kernel,
        (half, activations),
        [SMEM, ANY, VMEM] + any_weights,
        (VMEM, ANY),
        [token_blocks, weight_blocks, weight_blocks, token_blocks],
        4 * blocks,
        starts,
        upstream,
        slope,
        *weights,
    )
    arrived, input_grad = lax.optimization_barrier((arrived, input_grad))
    shadow_back = local_call(
        shadow_kernel,
        activations,
        [SMEM, ANY] + any_weights,
        ANY,
        [token_blocks, weight_blocks, weight_blocks, token_blocks],
        4 * blocks,
        starts,
        arrived,
        *weights,
    )
    shadow = over_section(shadow_back, -1)

    far_send = jnp.concatenate([cut(inputs, opposite), dpre], axis=1)
    dpre_send, far_send, out_pieces, shadow_back = lax.optimization_barrier(
        (dpre, far_send, out_pieces, shadow_back)
    )
    rights = [over_x(far_send if by == opposite else dpre_send, by) for by in steps]
    lefts = [
        rights[opposite - 1] if by == opposite else near_inputs[by] for by in steps
    ]
    in_pieces = [*lefts, *rights]
    ours = jnp.stack([x * wide + y * rows, y * rows]).astype(jnp.int32)
    apart = (1 - y) * rows
    other = jnp.stack([x * wide + apart, apart]).astype(jnp.int32)

    def part(where, kind, *arrays):
        return local_call(
            part_kernel,
            jax.ShapeDtypeStruct((rows, width), kind),
            [SMEM] + [ANY] * len(arrays),
            VMEM,
            [
                pltpu.VMEM((X_SIZE, tokens, rows), BF16),
                pltpu.VMEM((X_SIZE, tokens, width), BF16),
            ],
            2 * X_SIZE,
            where,
            *arrays,
        )

    received_out = swap_y(part(other, BF16, upstream, hidden, *out_pieces, *out_pieces))
    mine_out = part(ours, F32, upstream, hidden, *out_pieces, *out_pieces)
    shadow = local_call(
        copy_kernel,
        activations,
        [ANY],
        ANY,
        [pltpu.VMEM((tokens, features), BF16)],
        16,
        shadow,
    )
    in_pieces, mine_out = lax.optimization_barrier((in_pieces, mine_out))
    received_in = swap_y(part(other, BF16, inputs, dpre, *in_pieces))
    mine_in = part(ours, F32, inputs, dpre, *in_pieces)
    grad_out = mine_out + received_out.astype(F32)
    shadow, received_in = lax.optimization_barrier((shadow, received_in))
    grad_in = mine_in + received_in.astype(F32)
    return (
        layer_out[None],
        shadow[None],
        input_grad[None],
        grad_in[None],
        grad_out[None],
    )


def solution(mesh):
    spec = P("section", "dp", None)
    return jax.shard_map(
        on_device,
        mesh=mesh,
        in_specs=(spec,) * 4,
        out_specs=(spec,) * 5,
        check_vma=False,
    )
```

```python
import jax
import jax.numpy as jnp
from jax import lax
from jax.experimental import pallas as pl
from jax.experimental.pallas import tpu as pltpu
from jax.sharding import PartitionSpec as P

INV_ROOT_TWO = 0.7071067811865476
INV_ROOT_TWO_PI = 0.3989422804014327
X_SIZE = 4
Y_SIZE = 2
F32 = jnp.float32
BF16 = jnp.bfloat16


def over_section(array, by):
    devices = lax.axis_size("section")
    return lax.ppermute(
        array, "section", [(i, (i + by) % devices) for i in range(devices)]
    )


def over_x(array, by):
    pairs = []
    for x in range(X_SIZE):
        for y in range(Y_SIZE):
            pairs.append((x * Y_SIZE + y, ((x + by) % X_SIZE) * Y_SIZE + y))
    return lax.ppermute(array, "dp", pairs)


def swap_y(array):
    return lax.ppermute(array, "dp", [(i, i ^ 1) for i in range(X_SIZE * Y_SIZE)])


def gelu_pair(preact):
    normal_cdf = 0.5 * (1.0 + lax.erf(preact * INV_ROOT_TWO))
    density = jnp.exp(-0.5 * preact * preact) * INV_ROOT_TWO_PI
    return (preact * normal_cdf, normal_cdf + preact * density)


def times(left, right):
    return jnp.dot(left, right, preferred_element_type=F32)


def times_transposed(left, right):
    return lax.dot_general(
        left, right, (((1,), (1,)), ((), ())), preferred_element_type=F32
    )


def contract_tokens(left, right):
    return lax.dot_general(
        left, right, (((0,), (0,)), ((), ())), preferred_element_type=F32
    )


def weight_items(refs):
    near, far = refs[:6], refs[6:]
    rows = far[0].shape[0]
    items = [((ref, 0), (ref, rows)) for ref in near]
    items += [((far[k], 0), (far[k + 1], 0)) for k in range(0, len(far), 2)]
    return rows, items


def columns_of(starts, block, width):
    return pl.ds(pl.multiple_of(starts[block], width), width)


class Loads:
    def __init__(self, semaphores):
        self.semaphores, self.copies, self.waited = semaphores, [], set()

    def start(self, source, target):
        number = len(self.copies)
        copy = pltpu.make_async_copy(source, target, self.semaphores.at[number])
        copy.start()
        self.copies.append((copy, target))
        return number

    def get(self, number):
        copy, target = self.copies[number]
        if number not in self.waited:
            self.waited.add(number)
            copy.wait()
        return target

    def finish(self):
        for number in range(len(self.copies)):
            self.get(number)


def first_kernel(starts, inputs, *rest):
    (rows, items), rest = weight_items(rest[:8]), rest[8:]
    partial, left, up, semaphores = rest
    loads, numbers = Loads(semaphores), []
    for block, ((ref, row), _) in enumerate(items):
        columns = columns_of(starts, block, rows)
        numbers.append(
            (
                loads.start(inputs.at[:, columns], left.at[block]),
                loads.start(ref.at[pl.ds(row, rows)], up.at[block]),
            )
        )
    total = None
    for one, two in numbers:
        product = times(loads.get(one)[...], loads.get(two)[...])
        total = product if total is None else total + product
    partial[...] = total


def layer_kernel(starts, inputs, partial, *rest):
    (rows, items), rest = weight_items(rest[:10]), rest[10:]
    hidden, slope, output, left, up, down, result, semaphores = rest
    loads, lefts, downs = Loads(semaphores), [], []
    last = len(items) - 1
    order = [last, *range(last)]
    ref, row = items[last][0]
    up_number = loads.start(ref.at[pl.ds(row, rows)], up)
    for block in order:
        columns = columns_of(starts, block, rows)
        lefts.append(loads.start(inputs.at[:, columns], left.at[block]))
        ref, row = items[block][1]
        downs.append(loads.start(ref.at[pl.ds(row, rows)], down.at[block]))
    product = times(loads.get(lefts[0])[...], loads.get(up_number)[...])
    activated, gradient = gelu_pair(partial[...] + product)
    inner = activated.astype(BF16)
    hidden[...] = inner
    slope[...] = gradient
    for block, one, two in zip(order, lefts, downs):
        branch = times_transposed(inner, loads.get(two)[...])
        total = loads.get(one)[...].astype(F32) + branch
        result[block] = total.astype(BF16)
        loads.start(
            result.at[block], output.at[:, columns_of(starts, block, rows)]
        )
    loads.finish()


def back_kernel(starts, upstream, slope, *rest):
    (rows, items), rest = weight_items(rest[:10]), rest[10:]
    dpre, output, left, up, down, result, semaphores = rest
    loads, numbers, ups = Loads(semaphores), [], []
    for block, (_, (ref, row)) in enumerate(items):
        columns = columns_of(starts, block, rows)
        numbers.append(
            (
                loads.start(upstream.at[:, columns], left.at[block]),
                loads.start(ref.at[pl.ds(row, rows)], down.at[block]),
            )
        )
    for block, ((ref, row), _) in enumerate(items):
        ups.append(loads.start(ref.at[pl.ds(row, rows)], up.at[block]))
    dhidden = None
    for one, two in numbers:
        product = times(loads.get(one)[...], loads.get(two)[...])
        dhidden = product if dhidden is None else dhidden + product
    inner = (dhidden * slope[...]).astype(BF16)
    dpre[...] = inner
    for block, number in enumerate(ups):
        back = times_transposed(inner, loads.get(number)[...])
        total = left[block].astype(F32) + back
        result[block] = total.astype(BF16)
        loads.start(
            result.at[block], output.at[:, columns_of(starts, block, rows)]
        )
    loads.finish()


def shadow_kernel(starts, inputs, *rest):
    (rows, items), rest = weight_items(rest[:10]), rest[10:]
    output, left, up, down, result, semaphores = rest
    loads, numbers = Loads(semaphores), []
    for block, ((ref, row), _) in enumerate(items):
        columns = columns_of(starts, block, rows)
        numbers.append(
            (
                loads.start(inputs.at[:, columns], left.at[block]),
                loads.start(ref.at[pl.ds(row, rows)], up.at[block]),
            )
        )
    downs = []
    for block, (_, (ref, row)) in enumerate(items):
        downs.append(loads.start(ref.at[pl.ds(row, rows)], down.at[block]))
    preact = None
    for one, two in numbers:
        first = times(loads.get(one)[...], loads.get(two)[...])
        preact = first if preact is None else preact + first
    hidden = gelu_pair(preact)[0].astype(BF16)
    for block, number in enumerate(downs):
        branch = times_transposed(hidden, loads.get(number)[...])
        total = left[block].astype(F32) + branch
        result[block] = total.astype(BF16)
        loads.start(
            result.at[block], output.at[:, columns_of(starts, block, rows)]
        )
    loads.finish()


def part_kernel(starts, whole, other, *rest):
    pieces, (part, lefts, rights, semaphores) = rest[:-4], rest[-4:]
    rows, width = part.shape
    loads, numbers = Loads(semaphores), []
    numbers.append(
        (
            loads.start(whole.at[:, columns_of(starts, 0, rows)], lefts.at[0]),
            loads.start(other, rights.at[0]),
        )
    )
    count = len(pieces) // 2
    for k, (left, right) in enumerate(zip(pieces[:count], pieces[count:])):
        right = right.at[:, pl.ds(right.shape[1] - width, width)]
        numbers.append(
            (
                loads.start(
                    left.at[:, columns_of(starts, 1, rows)], lefts.at[k + 1]
                ),
                loads.start(right, rights.at[k + 1]),
            )
        )
    total = None
    for one, two in numbers:
        product = contract_tokens(loads.get(one)[...], loads.get(two)[...])
        total = product if total is None else total + product
    part[...] = total.astype(part.dtype)


def copy_kernel(source, target, held, semaphores):
    loads, count = Loads(semaphores), semaphores.shape[0] // 2
    rows = source.shape[0] // count
    for k in range(count):
        some = pl.ds(k * rows, rows)
        loads.start(source.at[some], held.at[some])
    for k in range(count):
        some = pl.ds(k * rows, rows)
        loads.get(k)
        loads.start(held.at[some], target.at[some])
    loads.finish()


ANY = pl.BlockSpec(memory_space=pl.ANY)
VMEM = pl.BlockSpec(memory_space=pltpu.VMEM)
SMEM = pl.BlockSpec(memory_space=pltpu.SMEM)


def local_call(kernel, outs, in_specs, out_specs, scratch, copies, *arrays):
    return pl.pallas_call(
        kernel,
        out_shape=outs,
        in_specs=in_specs,
        out_specs=out_specs,
        scratch_shapes=[*scratch, pltpu.SemaphoreType.DMA((copies,))],
        compiler_params=pltpu.CompilerParams(vmem_limit_bytes=56 * 2**20),
        cost_estimate=pl.CostEstimate(flops=1, bytes_accessed=1, transcendentals=0),
    )(*arrays)


def on_device(handoff, grad_back, w_in, w_out):
    position = lax.axis_index("dp")
    x, y = position // Y_SIZE, position % Y_SIZE
    rows, width = w_in.shape[1:]
    tokens, features = handoff.shape[1:]
    places = ((0, 0), (0, 1), (3, 0), (1, 0), (3, 1), (1, 1), (2, 0), (2, 1))
    starts = jnp.stack(
        [(lax.rem(x + i, X_SIZE) * Y_SIZE + (y + j) % Y_SIZE) * rows for i, j in places]
    ).astype(jnp.int32)

    own = jnp.concatenate([w_in[0], w_out[0]], axis=0)
    partner = swap_y(own)
    behind, ahead = over_x(own, 1), over_x(own, -1)
    handoff, partner, behind, ahead = lax.optimization_barrier(
        (handoff, partner, behind, ahead)
    )
    behind_partner, ahead_partner = over_x(partner, 1), over_x(partner, -1)
    far_in, far_out = over_x(behind[:rows], 1), over_x(ahead[rows:], -1)
    inputs = over_section(handoff[0], 1)
    far_partner_in = over_x(behind_partner[:rows], 1)
    far_partner_out = over_x(ahead_partner[rows:], -1)
    grad_back, inputs, _ = lax.optimization_barrier(
        (grad_back, inputs, (far_in, far_out, behind_partner, ahead_partner))
    )
    upstream = over_section(grad_back[0], -1)
    weights = (own, partner, behind, ahead, behind_partner, ahead_partner)
    weights += (far_in, far_out, far_partner_in, far_partner_out)

    blocks = X_SIZE * Y_SIZE
    activations = jax.ShapeDtypeStruct((tokens, features), BF16)
    half = jax.ShapeDtypeStruct((tokens, width), BF16)
    half_wide = jax.ShapeDtypeStruct((tokens, width), F32)
    token_blocks = pltpu.VMEM((blocks, tokens, rows), BF16)
    weight_blocks = pltpu.VMEM((blocks, rows, width), BF16)
    any_weights = [ANY] * len(weights)
    wide = Y_SIZE * rows

    def cut(array, by):
        first = lax.rem(x + by, X_SIZE) * wide
        return lax.dynamic_slice_in_dim(array, first, wide, axis=1)

    partial = local_call(
        first_kernel,
        half_wide,
        [SMEM, ANY] + [ANY] * 8,
        VMEM,
        [token_blocks, weight_blocks],
        2 * blocks,
        starts,
        inputs,
        *weights[:8],
    )
    hidden, slope, layer_out = local_call(
        layer_kernel,
        (half, half_wide, activations),
        [SMEM, ANY, VMEM] + any_weights,
        (VMEM, VMEM, ANY),
        [token_blocks, pltpu.VMEM((rows, width), BF16), weight_blocks, token_blocks],
        3 * blocks + 1,
        starts,
        inputs,
        partial,
        *weights,
    )
    steps = range(1, X_SIZE)
    opposite = X_SIZE // 2
    near_inputs = {by: over_x(cut(inputs, by), by) for by in steps if by != opposite}
    ready, near_inputs, upstream = lax.optimization_barrier(
        (layer_out, near_inputs, upstream)
    )
    arrived = over_section(ready, 1)
    out_pieces = [
        over_x(jnp.concatenate([cut(upstream, by), hidden], axis=1), by)
        for by in range(1, X_SIZE)
    ]
    dpre, input_grad = local_call(
        back_kernel,
        (half, activations),
        [SMEM, ANY, VMEM] + any_weights,
        (VMEM, ANY),
        [token_blocks, weight_blocks, weight_blocks, token_blocks],
        4 * blocks,
        starts,
        upstream,
        slope,
        *weights,
    )
    arrived, input_grad = lax.optimization_barrier((arrived, input_grad))
    shadow_back = local_call(
        shadow_kernel,
        activations,
        [SMEM, ANY] + any_weights,
        ANY,
        [token_blocks, weight_blocks, weight_blocks, token_blocks],
        4 * blocks,
        starts,
        arrived,
        *weights,
    )
    shadow = over_section(shadow_back, -1)

    far_send = jnp.concatenate([cut(inputs, opposite), dpre], axis=1)
    dpre_send, far_send, out_pieces, shadow_back = lax.optimization_barrier(
        (dpre, far_send, out_pieces, shadow_back)
    )
    rights = [over_x(far_send if by == opposite else dpre_send, by) for by in steps]
    lefts = [
        rights[opposite - 1] if by == opposite else near_inputs[by] for by in steps
    ]
    in_pieces = [*lefts, *rights]
    ours = jnp.stack([x * wide + y * rows, y * rows]).astype(jnp.int32)
    apart = (1 - y) * rows
    other = jnp.stack([x * wide + apart, apart]).astype(jnp.int32)

    def part(where, kind, *arrays):
        return local_call(
            part_kernel,
            jax.ShapeDtypeStruct((rows, width), kind),
            [SMEM] + [ANY] * len(arrays),
            VMEM,
            [
                pltpu.VMEM((X_SIZE, tokens, rows), BF16),
                pltpu.VMEM((X_SIZE, tokens, width), BF16),
            ],
            2 * X_SIZE,
            where,
            *arrays,
        )

    received_out = swap_y(part(other, BF16, upstream, hidden, *out_pieces, *out_pieces))
    mine_out = part(ours, F32, upstream, hidden, *out_pieces, *out_pieces)
    shadow = local_call(
        copy_kernel,
        activations,
        [ANY],
        ANY,
        [pltpu.VMEM((tokens, features), BF16)],
        16,
        shadow,
    )
    in_pieces, mine_out = lax.optimization_barrier((in_pieces, mine_out))
    received_in = swap_y(part(other, BF16, inputs, dpre, *in_pieces))
    mine_in = part(ours, F32, inputs, dpre, *in_pieces)
    grad_out = mine_out + received_out.astype(F32)
    shadow, received_in = lax.optimization_barrier((shadow, received_in))
    grad_in = mine_in + received_in.astype(F32)
    return (
        layer_out[None],
        shadow[None],
        input_grad[None],
        grad_in[None],
        grad_out[None],
    )


def solution(mesh):
    spec = P("section", "dp", None)
    return jax.shard_map(
        on_device,
        mesh=mesh,
        in_specs=(spec,) * 4,
        out_specs=(spec,) * 5,
        check_vma=False,
    )
```

```python
import jax
import jax.numpy as jnp
from jax import lax
from jax.experimental import pallas as pl
from jax.experimental.pallas import tpu as pltpu
from jax.sharding import PartitionSpec as P

INV_ROOT_TWO = 0.7071067811865476
INV_ROOT_TWO_PI = 0.3989422804014327
X_SIZE = 4
Y_SIZE = 2
F32 = jnp.float32
BF16 = jnp.bfloat16


def over_section(array, by):
    devices = lax.axis_size("section")
    return lax.ppermute(
        array, "section", [(i, (i + by) % devices) for i in range(devices)]
    )


def over_x(array, by):
    pairs = []
    for x in range(X_SIZE):
        for y in range(Y_SIZE):
            pairs.append((x * Y_SIZE + y, ((x + by) % X_SIZE) * Y_SIZE + y))
    return lax.ppermute(array, "dp", pairs)


def swap_y(array):
    return lax.ppermute(array, "dp", [(i, i ^ 1) for i in range(X_SIZE * Y_SIZE)])


def gelu_pair(preact):
    normal_cdf = 0.5 * (1.0 + lax.erf(preact * INV_ROOT_TWO))
    density = jnp.exp(-0.5 * preact * preact) * INV_ROOT_TWO_PI
    return (preact * normal_cdf, normal_cdf + preact * density)


def times(left, right):
    return jnp.dot(left, right, preferred_element_type=F32)


def times_transposed(left, right):
    return lax.dot_general(
        left, right, (((1,), (1,)), ((), ())), preferred_element_type=F32
    )


def contract_tokens(left, right):
    return lax.dot_general(
        left, right, (((0,), (0,)), ((), ())), preferred_element_type=F32
    )


def weight_items(refs):
    near, far = refs[:6], refs[6:]
    rows = far[0].shape[0]
    items = [((ref, 0), (ref, rows)) for ref in near]
    items += [((far[k], 0), (far[k + 1], 0)) for k in range(0, len(far), 2)]
    return rows, items


def columns_of(starts, block, width):
    return pl.ds(pl.multiple_of(starts[block], width), width)


class Loads:
    def __init__(self, semaphores):
        self.semaphores, self.copies, self.waited = semaphores, [], set()

    def start(self, source, target):
        number = len(self.copies)
        copy = pltpu.make_async_copy(source, target, self.semaphores.at[number])
        copy.start()
        self.copies.append((copy, target))
        return number

    def get(self, number):
        copy, target = self.copies[number]
        if number not in self.waited:
            self.waited.add(number)
            copy.wait()
        return target

    def finish(self):
        for number in range(len(self.copies)):
            self.get(number)


def first_kernel(starts, inputs, *rest):
    (rows, items), rest = weight_items(rest[:8]), rest[8:]
    partial, left, up, semaphores = rest
    loads, numbers = Loads(semaphores), []
    for block, ((ref, row), _) in enumerate(items):
        columns = columns_of(starts, block, rows)
        numbers.append(
            (
                loads.start(inputs.at[:, columns], left.at[block]),
                loads.start(ref.at[pl.ds(row, rows)], up.at[block]),
            )
        )
    total = None
    for one, two in numbers:
        product = times(loads.get(one)[...], loads.get(two)[...])
        total = product if total is None else total + product
    partial[...] = total


def layer_kernel(starts, inputs, partial, *rest):
    (rows, items), rest = weight_items(rest[:10]), rest[10:]
    hidden, slope, output, left, up, down, result, semaphores = rest
    loads, lefts, downs = Loads(semaphores), [], []
    last = len(items) - 1
    order = [last, *range(last)]
    ref, row = items[last][0]
    up_number = loads.start(ref.at[pl.ds(row, rows)], up)
    for block in order:
        columns = columns_of(starts, block, rows)
        lefts.append(loads.start(inputs.at[:, columns], left.at[block]))
        ref, row = items[block][1]
        downs.append(loads.start(ref.at[pl.ds(row, rows)], down.at[block]))
    product = times(loads.get(lefts[0])[...], loads.get(up_number)[...])
    activated, gradient = gelu_pair(partial[...] + product)
    inner = activated.astype(BF16)
    hidden[...] = inner
    slope[...] = gradient
    for block, one, two in zip(order, lefts, downs):
        branch = times_transposed(inner, loads.get(two)[...])
        total = loads.get(one)[...].astype(F32) + branch
        result[block] = total.astype(BF16)
        loads.start(
            result.at[block], output.at[:, columns_of(starts, block, rows)]
        )
    loads.finish()


def back_kernel(starts, upstream, slope, *rest):
    (rows, items), rest = weight_items(rest[:10]), rest[10:]
    dpre, output, left, up, down, result, semaphores = rest
    loads, numbers, ups = Loads(semaphores), [], []
    for block, (_, (ref, row)) in enumerate(items):
        columns = columns_of(starts, block, rows)
        numbers.append(
            (
                loads.start(upstream.at[:, columns], left.at[block]),
                loads.start(ref.at[pl.ds(row, rows)], down.at[block]),
            )
        )
    for block, ((ref, row), _) in enumerate(items):
        ups.append(loads.start(ref.at[pl.ds(row, rows)], up.at[block]))
    dhidden = None
    for one, two in numbers:
        product = times(loads.get(one)[...], loads.get(two)[...])
        dhidden = product if dhidden is None else dhidden + product
    inner = (dhidden * slope[...]).astype(BF16)
    dpre[...] = inner
    for block, number in enumerate(ups):
        back = times_transposed(inner, loads.get(number)[...])
        total = left[block].astype(F32) + back
        result[block] = total.astype(BF16)
        loads.start(
            result.at[block], output.at[:, columns_of(starts, block, rows)]
        )
    loads.finish()


def shadow_kernel(starts, inputs, *rest):
    (rows, items), rest = weight_items(rest[:10]), rest[10:]
    output, left, up, down, result, semaphores = rest
    loads, numbers = Loads(semaphores), []
    for block, ((ref, row), _) in enumerate(items):
        columns = columns_of(starts, block, rows)
        numbers.append(
            (
                loads.start(inputs.at[:, columns], left.at[block]),
                loads.start(ref.at[pl.ds(row, rows)], up.at[block]),
            )
        )
    downs = []
    for block, (_, (ref, row)) in enumerate(items):
        downs.append(loads.start(ref.at[pl.ds(row, rows)], down.at[block]))
    preact = None
    for one, two in numbers:
        first = times(loads.get(one)[...], loads.get(two)[...])
        preact = first if preact is None else preact + first
    hidden = gelu_pair(preact)[0].astype(BF16)
    for block, number in enumerate(downs):
        branch = times_transposed(hidden, loads.get(number)[...])
        total = left[block].astype(F32) + branch
        result[block] = total.astype(BF16)
        loads.start(
            result.at[block], output.at[:, columns_of(starts, block, rows)]
        )
    loads.finish()


def part_kernel(starts, whole, other, *rest):
    pieces, (part, lefts, rights, semaphores) = rest[:-4], rest[-4:]
    rows, width = part.shape
    loads, numbers = Loads(semaphores), []
    numbers.append(
        (
            loads.start(whole.at[:, columns_of(starts, 0, rows)], lefts.at[0]),
            loads.start(other, rights.at[0]),
        )
    )
    for k, piece in enumerate(pieces):
        right = piece.at[:, pl.ds(piece.shape[1] - width, width)]
        numbers.append(
            (
                loads.start(
                    piece.at[:, columns_of(starts, 1, rows)], lefts.at[k + 1]
                ),
                loads.start(right, rights.at[k + 1]),
            )
        )
    total = None
    for one, two in numbers:
        product = contract_tokens(loads.get(one)[...], loads.get(two)[...])
        total = product if total is None else total + product
    part[...] = total.astype(part.dtype)


def copy_kernel(source, target, held, semaphores):
    loads, count = Loads(semaphores), semaphores.shape[0] // 2
    rows = source.shape[0] // count
    for k in range(count):
        some = pl.ds(k * rows, rows)
        loads.start(source.at[some], held.at[some])
    for k in range(count):
        some = pl.ds(k * rows, rows)
        loads.get(k)
        loads.start(held.at[some], target.at[some])
    loads.finish()


ANY = pl.BlockSpec(memory_space=pl.ANY)
VMEM = pl.BlockSpec(memory_space=pltpu.VMEM)
SMEM = pl.BlockSpec(memory_space=pltpu.SMEM)


def local_call(kernel, outs, in_specs, out_specs, scratch, copies, *arrays):
    return pl.pallas_call(
        kernel,
        out_shape=outs,
        in_specs=in_specs,
        out_specs=out_specs,
        scratch_shapes=[*scratch, pltpu.SemaphoreType.DMA((copies,))],
        compiler_params=pltpu.CompilerParams(vmem_limit_bytes=56 * 2**20),
        cost_estimate=pl.CostEstimate(flops=1, bytes_accessed=1, transcendentals=0),
    )(*arrays)


def on_device(handoff, grad_back, w_in, w_out):
    position = lax.axis_index("dp")
    x, y = position // Y_SIZE, position % Y_SIZE
    rows, width = w_in.shape[1:]
    tokens, features = handoff.shape[1:]
    places = ((0, 0), (0, 1), (3, 0), (1, 0), (3, 1), (1, 1), (2, 0), (2, 1))
    starts = jnp.stack(
        [(lax.rem(x + i, X_SIZE) * Y_SIZE + (y + j) % Y_SIZE) * rows for i, j in places]
    ).astype(jnp.int32)

    own = jnp.concatenate([w_in[0], w_out[0]], axis=0)
    partner = swap_y(own)
    behind, ahead = over_x(own, 1), over_x(own, -1)
    handoff, partner, behind, ahead = lax.optimization_barrier(
        (handoff, partner, behind, ahead)
    )
    behind_partner, ahead_partner = over_x(partner, 1), over_x(partner, -1)
    far_in, far_out = over_x(behind[:rows], 1), over_x(ahead[rows:], -1)
    inputs = over_section(handoff[0], 1)
    far_partner_in = over_x(behind_partner[:rows], 1)
    far_partner_out = over_x(ahead_partner[rows:], -1)
    grad_back, inputs = lax.optimization_barrier((grad_back, inputs))
    upstream = over_section(grad_back[0], -1)
    weights = (own, partner, behind, ahead, behind_partner, ahead_partner)
    weights += (far_in, far_out, far_partner_in, far_partner_out)

    blocks = X_SIZE * Y_SIZE
    activations = jax.ShapeDtypeStruct((tokens, features), BF16)
    half = jax.ShapeDtypeStruct((tokens, width), BF16)
    half_wide = jax.ShapeDtypeStruct((tokens, width), F32)
    token_blocks = pltpu.VMEM((blocks, tokens, rows), BF16)
    weight_blocks = pltpu.VMEM((blocks, rows, width), BF16)
    any_weights = [ANY] * len(weights)
    wide = Y_SIZE * rows

    def cut(array, by):
        first = lax.rem(x + by, X_SIZE) * wide
        return lax.dynamic_slice_in_dim(array, first, wide, axis=1)

    partial = local_call(
        first_kernel,
        half_wide,
        [SMEM, ANY] + [ANY] * 8,
        VMEM,
        [token_blocks, weight_blocks],
        2 * blocks,
        starts,
        inputs,
        *weights[:8],
    )
    hidden, slope, layer_out = local_call(
        layer_kernel,
        (half, half_wide, activations),
        [SMEM, ANY, VMEM] + any_weights,
        (VMEM, VMEM, ANY),
        [token_blocks, pltpu.VMEM((rows, width), BF16), weight_blocks, token_blocks],
        3 * blocks + 1,
        starts,
        inputs,
        partial,
        *weights,
    )
    arrived = over_section(layer_out, 1)
    out_pieces = [
        over_x(jnp.concatenate([cut(upstream, by), hidden], axis=1), by)
        for by in range(1, X_SIZE)
    ]
    dpre, input_grad = local_call(
        back_kernel,
        (half, activations),
        [SMEM, ANY, VMEM] + any_weights,
        (VMEM, ANY),
        [token_blocks, weight_blocks, weight_blocks, token_blocks],
        4 * blocks,
        starts,
        upstream,
        slope,
        *weights,
    )
    arrived, input_grad = lax.optimization_barrier((arrived, input_grad))
    shadow_back = local_call(
        shadow_kernel,
        activations,
        [SMEM, ANY] + any_weights,
        ANY,
        [token_blocks, weight_blocks, weight_blocks, token_blocks],
        4 * blocks,
        starts,
        arrived,
        *weights,
    )
    shadow = over_section(shadow_back, -1)

    in_pieces = [
        jnp.concatenate([cut(inputs, by), dpre], axis=1) for by in range(1, X_SIZE)
    ]
    in_pieces, out_pieces, shadow_back = lax.optimization_barrier(
        (in_pieces, out_pieces, shadow_back)
    )
    in_pieces = [over_x(piece, by + 1) for by, piece in enumerate(in_pieces)]
    ours = jnp.stack([x * wide + y * rows, y * rows]).astype(jnp.int32)
    apart = (1 - y) * rows
    other = jnp.stack([x * wide + apart, apart]).astype(jnp.int32)

    def part(where, kind, *arrays):
        return local_call(
            part_kernel,
            jax.ShapeDtypeStruct((rows, width), kind),
            [SMEM] + [ANY] * len(arrays),
            VMEM,
            [
                pltpu.VMEM((X_SIZE, tokens, rows), BF16),
                pltpu.VMEM((X_SIZE, tokens, width), BF16),
            ],
            2 * X_SIZE,
            where,
            *arrays,
        )

    received_out = swap_y(part(other, BF16, upstream, hidden, *out_pieces))
    mine_out = part(ours, F32, upstream, hidden, *out_pieces)
    shadow = local_call(
        copy_kernel,
        activations,
        [ANY],
        ANY,
        [pltpu.VMEM((tokens, features), BF16)],
        16,
        shadow,
    )
    in_pieces, mine_out = lax.optimization_barrier((in_pieces, mine_out))
    received_in = swap_y(part(other, BF16, inputs, dpre, *in_pieces))
    mine_in = part(ours, F32, inputs, dpre, *in_pieces)
    grad_out = mine_out + received_out.astype(F32)
    shadow, received_in = lax.optimization_barrier((shadow, received_in))
    grad_in = mine_in + received_in.astype(F32)
    return (
        layer_out[None],
        shadow[None],
        input_grad[None],
        grad_in[None],
        grad_out[None],
    )


def solution(mesh):
    spec = P("section", "dp", None)
    return jax.shard_map(
        on_device,
        mesh=mesh,
        in_specs=(spec,) * 4,
        out_specs=(spec,) * 5,
        check_vma=False,
    )
```
